512 devices in a mesh: rep: 8 (over x, core), fsdp: 64 (over z, y).
Axes of the slice: x: 4, y: 4, z: 16, core: 2. Of those that a mesh axis runs over, the one named last changes fastest.
Arguments:
- partials: bfloat16 [8, 16, 512, 4096], P('rep', None, 'fsdp'), may hold values from -5 to 5
- left_basis: bfloat16 [8, 64, 512, 512], P('rep', 'fsdp'), may hold values from -0.25 to 0.25
- right_basis: bfloat16 [8, 64, 512, 512], P('rep', 'fsdp'), may hold values from -0.25 to 0.25
- first_moment: bfloat16 [8, 64, 512, 512], P('rep', 'fsdp'), may hold values from -4 to 4
- second_moment: bfloat16 [8, 64, 512, 512], P('rep', 'fsdp'), may hold values from 0.099609375 to 2
- owners: int32 [8, 16], replicated, may hold values from 0 to 63, as said below
Outputs:
- first_new: bfloat16 [8, 64, 512, 512], P('rep', 'fsdp')
- second_new: bfloat16 [8, 64, 512, 512], P('rep', 'fsdp')
- update: bfloat16 [16, 512, 4096], P(None, 'fsdp', 'rep')
The draws below stay inside these ranges and needn't reach their ends.
Inputs may be any that keep to these rules, and one draw needn't show every extreme that they name: Within each row of owners the 16 entries are distinct; each row contains 0 and 64 - 1.
All inputs are finite; a program needn't handle non-finite values.
Results may differ from the reference program's by a relative error of at most 0.015.
Values may be sent and summed in bfloat16 or wider, within the bound.
No kernel may reach another device: no remote copies, remote signals or barrier semaphores. Data moves between devices by JAX's collectives and lax.ppermute only.
A program may use at most 64 MiB of HBM per device.

```python
import math
import jax
import jax.numpy as jnp
from jax import lax

D = 4096
BLOCK = 512
RBLK = 16
CBLK = 1
NBLK = 16
N_REP = 8
N_FSDP = 64


def draw_owners(key, part):
    key = jax.random.fold_in(key, 11)

    def one_row(row_key):
        first_key, second_key = jax.random.split(row_key)
        middle = jax.random.permutation(first_key, N_FSDP - 2) + 1
        chosen = jnp.concatenate([jnp.array([0, N_FSDP - 1], jnp.int32), middle[:NBLK - 2].astype(jnp.int32)])
        return chosen[jax.random.permutation(second_key, NBLK)]
    return jax.vmap(one_row)(jax.random.split(key, N_REP)).astype(jnp.int32)


def steps_of(own_key, shape, cuts, smallest, high):
    factor_of, own = 1.0, jax.random.fold_in(own_key, 6)
    for dim, parts in cuts:
        draws = jnp.exp(jax.random.uniform(jax.random.fold_in(own, dim), (parts,), jnp.float32, smallest / len(cuts), high / len(cuts)))
        factor_of = factor_of * jnp.repeat(draws, shape[dim] // parts).reshape([-1 if axis == dim else 1 for axis in range(len(shape))])
    return factor_of


def gaussian(key, extent, scale, limit, cuts=(), held_as=jnp.bfloat16):
    values = scale * jax.random.normal(key, extent, jnp.float32)
    if cuts:
        values = values * steps_of(key, extent, cuts, -0.22, 0.18)
    return jnp.clip(values, -limit, limit).astype(held_as)


def setup_inputs(seed: int = 0) -> dict:
    key_of = jax.random.split(jax.random.key(seed), 7)
    return {
        "partials": gaussian(key_of[0], (N_REP, RBLK, BLOCK, D), 0.35, 5.0, ((0, 8), (2, 64))),
        "left_basis": gaussian(key_of[1], (N_REP, N_FSDP, BLOCK, BLOCK), BLOCK ** -0.5, 0.25, ((0, 8), (1, 64))),
        "right_basis": gaussian(key_of[2], (N_REP, N_FSDP, BLOCK, BLOCK), BLOCK ** -0.5, 0.25, ((0, 8), (1, 64))),
        "first_moment": gaussian(key_of[3], (N_REP, N_FSDP, BLOCK, BLOCK), 0.3, 4.0, ((0, 8), (1, 64))),
        "second_moment": jnp.clip(jnp.exp(math.log(2.0) - 2.9996462 * jax.random.uniform(key_of[4], (N_REP, N_FSDP, BLOCK, BLOCK), jnp.float32) ** steps_of(key_of[4], (N_REP, N_FSDP, BLOCK, BLOCK), ((0, 8), (1, 64)), -0.2, 0.2)), 0.099609375, 2.0).astype(jnp.bfloat16),
        "owners": draw_owners(jax.random.fold_in(key_of[6], 71), 0),
    }


def per_group(group_args):
    grad_blocks, left_group, right_group, first_group, second_group, owner_row = group_args
    left_owned = left_group[owner_row].astype(jnp.float32)
    right_owned = right_group[owner_row].astype(jnp.float32)
    rotated_left = jnp.einsum('nxi,nxj->nij', left_owned, grad_blocks.astype(jnp.float32)).astype(jnp.bfloat16)
    rotated_blocks = jnp.einsum('nij,njk->nik', rotated_left.astype(jnp.float32), right_owned)
    rotated = jnp.zeros((N_FSDP, BLOCK, BLOCK), jnp.float32).at[owner_row].set(rotated_blocks)
    moment_one = 0.95 * first_group.astype(jnp.float32) + 0.05 * rotated
    moment_two = 0.95 * second_group.astype(jnp.float32) + 0.05 * rotated * rotated
    step_ratio = (moment_one[owner_row] / (jnp.sqrt(moment_two[owner_row]) + 1e-08)).astype(jnp.bfloat16)
    back_left = jnp.einsum('nij,njk->nik', left_owned, step_ratio.astype(jnp.float32)).astype(jnp.bfloat16)
    block_update = jnp.einsum('nik,nlk->nil', back_left.astype(jnp.float32), right_owned).astype(jnp.bfloat16)
    return (moment_one.astype(jnp.bfloat16), moment_two.astype(jnp.bfloat16), block_update)

def reference(partials, left_basis, right_basis, first_moment, second_moment, owners):
    gradient = lax.optimization_barrier(jnp.sum(partials.astype(jnp.float32), axis=0)).astype(jnp.bfloat16)
    blocks = gradient.reshape(RBLK, BLOCK, N_REP, CBLK, BLOCK).transpose(2, 0, 3, 1, 4).reshape(N_REP, NBLK, BLOCK, BLOCK)
    first_new, second_new, updates = lax.map(per_group, (blocks, left_basis, right_basis, first_moment, second_moment, owners))
    update = updates.reshape(N_REP, RBLK, CBLK, BLOCK, BLOCK).transpose(1, 3, 0, 2, 4).reshape(RBLK, BLOCK, D)
    return (first_new, second_new, update)
```

```python
import jax
import jax.numpy as jnp
from jax import lax
from jax.experimental import pallas as pl
from jax.experimental.pallas import tpu as pltpu
from jax.sharding import PartitionSpec as P

N_REP = 8
N_FSDP = 64
SUB = 8
SIDE = 512
BLOCKS = 16
STRIP = 128

FIRST = N_FSDP // 2
ORDER = [(p + FIRST) % N_FSDP for p in range(N_FSDP)]


def hbm():
    return pl.BlockSpec(memory_space=pl.ANY)


def vmem():
    return pl.BlockSpec(memory_space=pltpu.VMEM)


def cut_kernel(partials, blocks, held, in_sems, out_sems):
    loads = [
        pltpu.make_async_copy(
            partials.at[0, :, :, pl.ds(r * SIDE, SIDE)], held.at[r], in_sems.at[r]
        )
        for r in range(N_REP)
    ]
    stores = [
        pltpu.make_async_copy(held.at[r], blocks.at[r], out_sems.at[r]) for r in range(N_REP)
    ]
    for c in loads:
        c.start()
    for load, store in zip(loads, stores):
        load.wait()
        store.start()
    for c in stores:
        c.wait()


def cut_columns(partials):
    shape = (N_REP, BLOCKS, SUB, SIDE)
    return pl.pallas_call(
        cut_kernel,
        out_shape=jax.ShapeDtypeStruct(shape, jnp.bfloat16),
        in_specs=[hbm()],
        out_specs=hbm(),
        scratch_shapes=[
            pltpu.VMEM(shape, jnp.bfloat16),
            pltpu.SemaphoreType.DMA((N_REP,)),
            pltpu.SemaphoreType.DMA((N_REP,)),
        ],
        name="cut_columns",
    )(partials)


def step_kernel(
    grad, left, left_turned, right, right_turned, first, second,
    first_new_hbm, second_new_hbm, block_update,
    first_new, second_new, ratio, sems,
):
    turned = jnp.dot(left_turned[...], grad[...], preferred_element_type=jnp.float32).astype(
        jnp.bfloat16
    )
    for i in range(SIDE // STRIP):
        rows = slice(i * STRIP, (i + 1) * STRIP)
        rotated = jnp.dot(turned[rows], right[...], preferred_element_type=jnp.float32)
        one = 0.95 * first[rows, :].astype(jnp.float32) + 0.05 * rotated
        two = 0.95 * second[rows, :].astype(jnp.float32) + 0.05 * rotated * rotated
        first_new[rows, :] = one.astype(jnp.bfloat16)
        second_new[rows, :] = two.astype(jnp.bfloat16)
        ratio[rows, :] = (one / (jnp.sqrt(two) + 1e-08)).astype(jnp.bfloat16)
    stores = [
        pltpu.make_async_copy(first_new, first_new_hbm, sems.at[0]),
        pltpu.make_async_copy(second_new, second_new_hbm, sems.at[1]),
    ]
    for c in stores:
        c.start()
    back = jnp.dot(left[...], ratio[...], preferred_element_type=jnp.float32).astype(jnp.bfloat16)
    block_update[...] = jnp.dot(
        back, right_turned[...], preferred_element_type=jnp.float32
    ).astype(jnp.bfloat16)
    for c in stores:
        c.wait()


def step(*operands):
    square = jax.ShapeDtypeStruct((SIDE, SIDE), jnp.bfloat16)
    return pl.pallas_call(
        step_kernel,
        out_shape=(square, square, square),
        in_specs=[vmem()] * 7,
        out_specs=(hbm(), hbm(), vmem()),
        scratch_shapes=[pltpu.VMEM((SIDE, SIDE), jnp.bfloat16)] * 3 + [pltpu.SemaphoreType.DMA((2,))],
        compiler_params=pltpu.CompilerParams(vmem_limit_bytes=24 * 1024 * 1024),
        cost_estimate=pl.CostEstimate(
            flops=8 * SIDE**3, bytes_accessed=18 * SIDE**2, transcendentals=2 * SIDE**2
        ),
        name="soap_step",
    )(*operands)


def exchange(pieces):
    return lax.all_to_all(pieces, "fsdp", 0, 0, axis_index_groups=[ORDER], tiled=True)


def local(partials, left_basis, right_basis, first_moment, second_moment, owners):
    owner_row = lax.dynamic_slice_in_dim(owners, lax.axis_index("rep"), 1, 0)[0]
    places = lax.rem(owner_row + (N_FSDP - FIRST), N_FSDP)
    slots = jnp.arange(N_FSDP, dtype=jnp.int32)
    selector = (places[None, :] == slots[:, None]).astype(jnp.bfloat16)

    parts = lax.all_to_all(cut_columns(partials), "rep", 0, 0, tiled=True)
    right = right_basis[0, 0]
    left = jnp.roll(left_basis[0, 0], -FIRST * SUB, 0)
    parts, left, left_turned, right_turned, selector = lax.optimization_barrier(
        (parts, left, left.T, right.T, selector)
    )
    pieces = jnp.sum(parts.astype(jnp.float32), axis=0).astype(jnp.bfloat16)
    outgoing = jnp.einsum(
        "qb,bsk->qsk", selector, pieces, preferred_element_type=jnp.float32
    ).astype(jnp.bfloat16)
    arrived = exchange(outgoing)
    first_new, second_new, block_update = step(
        arrived.reshape(SIDE, SIDE), left, left_turned, right, right_turned,
        first_moment[0, 0], second_moment[0, 0],
    )
    returned = exchange(block_update.reshape(N_FSDP, SUB, SIDE))
    update = jnp.einsum(
        "qb,qsk->bsk", selector, returned, preferred_element_type=jnp.float32
    ).astype(jnp.bfloat16)
    return (first_new[None, None], second_new[None, None], update)


def solution(mesh):
    return jax.shard_map(
        local,
        mesh=mesh,
        in_specs=(
            P("rep", None, "fsdp", None),
            P("rep", "fsdp", None, None),
            P("rep", "fsdp", None, None),
            P("rep", "fsdp", None, None),
            P("rep", "fsdp", None, None),
            P(),
        ),
        out_specs=(
            P("rep", "fsdp", None, None),
            P("rep", "fsdp", None, None),
            P(None, "fsdp", "rep"),
        ),
        check_vma=False,
    )
```

```python
import jax
import jax.numpy as jnp
from jax import lax
from jax.experimental import pallas as pl
from jax.experimental.pallas import tpu as pltpu
from jax.sharding import PartitionSpec as P

N_X = 4
N_Y = 4
N_Z = 16
N_FSDP = N_Z * N_Y
SUB = 8
SIDE = 512
BLOCKS = 16
STRIP = 128

PLANES = [8, 0, 1, 15, 2, 14, 3, 13, 4, 12, 5, 11, 6, 10, 7, 9]
ORDER = [z * N_Y + (y + N_Y // 2) % N_Y for z in PLANES for y in range(N_Y)]
PAIR = 2 * SUB


def chip_of(p):
    return (p + N_X // 2) % N_X


def hbm():
    return pl.BlockSpec(memory_space=pl.ANY)


def vmem():
    return pl.BlockSpec(memory_space=pltpu.VMEM)


def pair_kernel(own, other, pair):
    core = lax.rem(lax.axis_index("rep"), 2)
    for p in range(N_X):
        columns = pl.ds(pl.multiple_of((2 * chip_of(p) + core) * SIDE, SIDE), SIDE)
        total = own[:, :, columns].astype(jnp.float32) + other[:, :, columns].astype(jnp.float32)
        pair[p] = total.astype(jnp.bfloat16)


def add_pair(own, other):
    return pl.pallas_call(
        pair_kernel,
        out_shape=jax.ShapeDtypeStruct((N_X, BLOCKS, SUB, SIDE), jnp.bfloat16),
        in_specs=[vmem(), vmem()],
        out_specs=vmem(),
        compiler_params=pltpu.CompilerParams(vmem_limit_bytes=16 * 1024 * 1024),
        name="add_pair",
    )(own, other)


def step_kernel(
    arrived, left, left_turned, right, right_turned, first, second,
    first_new_hbm, second_new_hbm, leaving,
    grad, first_new, second_new, ratio, sems,
):
    places = [
        (slice(p * SUB, p * SUB + PAIR), slice(ORDER[p] * SUB, ORDER[p] * SUB + PAIR))
        for p in range(0, N_FSDP, 2)
    ]
    for here, natural in places:
        grad[natural, :] = arrived[here, :]
    turned = jnp.dot(left_turned[...], grad[...], preferred_element_type=jnp.float32).astype(
        jnp.bfloat16
    )
    for i in range(SIDE // STRIP):
        rows = slice(i * STRIP, (i + 1) * STRIP)
        rotated = jnp.dot(turned[rows], right[...], preferred_element_type=jnp.float32)
        one = 0.95 * first[rows, :].astype(jnp.float32) + 0.05 * rotated
        two = 0.95 * second[rows, :].astype(jnp.float32) + 0.05 * rotated * rotated
        first_new[rows, :] = one.astype(jnp.bfloat16)
        second_new[rows, :] = two.astype(jnp.bfloat16)
        ratio[rows, :] = (one / (jnp.sqrt(two) + 1e-08)).astype(jnp.bfloat16)
    stores = [
        pltpu.make_async_copy(first_new, first_new_hbm, sems.at[0]),
        pltpu.make_async_copy(second_new, second_new_hbm, sems.at[1]),
    ]
    for c in stores:
        c.start()
    back = jnp.dot(left[...], ratio[...], preferred_element_type=jnp.float32).astype(jnp.bfloat16)
    block_update = jnp.dot(back, right_turned[...], preferred_element_type=jnp.float32).astype(
        jnp.bfloat16
    )
    for here, natural in places:
        leaving[here, :] = block_update[natural, :]
    for c in stores:
        c.wait()


def step(*operands):
    square = jax.ShapeDtypeStruct((SIDE, SIDE), jnp.bfloat16)
    return pl.pallas_call(
        step_kernel,
        out_shape=(square, square, square),
        in_specs=[vmem()] * 7,
        out_specs=(hbm(), hbm(), vmem()),
        scratch_shapes=[pltpu.VMEM((SIDE, SIDE), jnp.bfloat16)] * 4 + [pltpu.SemaphoreType.DMA((2,))],
        compiler_params=pltpu.CompilerParams(vmem_limit_bytes=24 * 1024 * 1024),
        cost_estimate=pl.CostEstimate(
            flops=8 * SIDE**3, bytes_accessed=18 * SIDE**2, transcendentals=2 * SIDE**2
        ),
        name="soap_step",
    )(*operands)


def exchange(pieces):
    return lax.all_to_all(pieces, "fsdp", 0, 0, axis_index_groups=[ORDER], tiled=True)


def local(partials, left_basis, right_basis, first_moment, second_moment, owners):
    owner_row = lax.dynamic_slice_in_dim(owners, lax.axis_index("rep"), 1, 0)[0]
    slots = jnp.array(ORDER, jnp.int32)
    selector = (owner_row[None, :] == slots[:, None]).astype(jnp.bfloat16)
    left = left_basis[0, 0]
    right = right_basis[0, 0]

    own = partials[0]
    other = lax.ppermute(own, "rep", [(i, i ^ 1) for i in range(2 * N_X)])
    other, left_turned, right_turned, selector = lax.optimization_barrier(
        (other, left.T, right.T, selector)
    )
    pair = add_pair(own, other)
    chips = [[2 * chip_of(p) + core for p in range(N_X)] for core in range(2)]
    parts = lax.all_to_all(pair, "rep", 0, 0, axis_index_groups=chips, tiled=True)
    pieces = jnp.sum(parts.astype(jnp.float32), axis=0).astype(jnp.bfloat16)

    outgoing = jnp.einsum(
        "qb,bsk->qsk", selector, pieces, preferred_element_type=jnp.float32
    ).astype(jnp.bfloat16)
    arrived = exchange(outgoing)
    first_new, second_new, leaving = step(
        arrived.reshape(SIDE, SIDE), left, left_turned, right, right_turned,
        first_moment[0, 0], second_moment[0, 0],
    )
    returned = exchange(leaving.reshape(N_FSDP, SUB, SIDE))
    update = jnp.einsum(
        "qb,qsk->bsk", selector, returned, preferred_element_type=jnp.float32
    ).astype(jnp.bfloat16)
    return (first_new[None, None], second_new[None, None], update)


def solution(mesh):
    return jax.shard_map(
        local,
        mesh=mesh,
        in_specs=(
            P("rep", None, "fsdp", None),
            P("rep", "fsdp", None, None),
            P("rep", "fsdp", None, None),
            P("rep", "fsdp", None, None),
            P("rep", "fsdp", None, None),
            P(),
        ),
        out_specs=(
            P("rep", "fsdp", None, None),
            P("rep", "fsdp", None, None),
            P(None, "fsdp", "rep"),
        ),
        check_vma=False,
    )
```

```python
import jax
import jax.numpy as jnp
from jax import lax
from jax.experimental import pallas as pl
from jax.experimental.pallas import tpu as pltpu
from jax.sharding import PartitionSpec as P

N_X = 4
N_Y = 4
N_Z = 16
N_FSDP = N_Z * N_Y
SUB = 8
SIDE = 512
BLOCKS = 16
STRIP = 128

def natural_of(p):
    return (p // N_Y + N_Z // 2) % N_Z * N_Y + (p % N_Y + N_Y // 2) % N_Y


def chip_of(p):
    return (p + N_X // 2) % N_X


ORDER = [natural_of(p) for p in range(N_FSDP)]
PAIR = 2 * SUB


def hbm():
    return pl.BlockSpec(memory_space=pl.ANY)


def vmem():
    return pl.BlockSpec(memory_space=pltpu.VMEM)


def pair_kernel(own, other, *refs):
    pair = refs[-1]
    core = lax.rem(lax.axis_index("rep"), 2)
    for p in range(N_X):
        columns = pl.ds(pl.multiple_of((2 * chip_of(p) + core) * SIDE, SIDE), SIDE)
        total = own[:, :, columns].astype(jnp.float32) + other[:, :, columns].astype(jnp.float32)
        pair[p] = total.astype(jnp.bfloat16)


def add_pair(own, other, *after):
    return pl.pallas_call(
        pair_kernel,
        out_shape=jax.ShapeDtypeStruct((N_X, BLOCKS, SUB, SIDE), jnp.bfloat16),
        in_specs=[vmem(), vmem()] + [vmem()] * len(after),
        out_specs=vmem(),
        compiler_params=pltpu.CompilerParams(vmem_limit_bytes=16 * 1024 * 1024),
        name="add_pair",
    )(own, other, *after)


def place_kernel(places, pieces, outgoing):
    outgoing[...] = jnp.zeros_like(outgoing)
    for b in range(BLOCKS):
        outgoing[places[b]] = pieces[b]


def place_blocks(places, pieces):
    return pl.pallas_call(
        place_kernel,
        out_shape=jax.ShapeDtypeStruct((N_FSDP, SUB, SIDE), jnp.bfloat16),
        in_specs=[pl.BlockSpec(memory_space=pltpu.SMEM), vmem()],
        out_specs=vmem(),
        compiler_params=pltpu.CompilerParams(vmem_limit_bytes=16 * 1024 * 1024),
        name="place_blocks",
    )(places, pieces)


def pick_kernel(places, returned, update, sems):
    copies = [
        pltpu.make_async_copy(returned.at[places[b]], update.at[b], sems.at[b])
        for b in range(BLOCKS)
    ]
    for c in copies:
        c.start()
    for c in copies:
        c.wait()


def pick_blocks(places, returned):
    return pl.pallas_call(
        pick_kernel,
        out_shape=jax.ShapeDtypeStruct((BLOCKS, SUB, SIDE), jnp.bfloat16),
        in_specs=[pl.BlockSpec(memory_space=pltpu.SMEM), vmem()],
        out_specs=hbm(),
        scratch_shapes=[pltpu.SemaphoreType.DMA((BLOCKS,))],
        compiler_params=pltpu.CompilerParams(vmem_limit_bytes=16 * 1024 * 1024),
        name="pick_blocks",
    )(places, returned)


def step_kernel(
    arrived, left, left_turned, right, first, second,
    first_new_hbm, second_new_hbm, leaving,
    grad, first_new, second_new, ratio, sems,
):
    places = [
        (slice(p * SUB, p * SUB + PAIR), slice(ORDER[p] * SUB, ORDER[p] * SUB + PAIR))
        for p in range(0, N_FSDP, 2)
    ]
    for here, natural in places:
        grad[natural, :] = arrived[here, :]
    turned = jnp.dot(left_turned[...], grad[...], preferred_element_type=jnp.float32).astype(
        jnp.bfloat16
    )
    for i in range(SIDE // STRIP):
        rows = slice(i * STRIP, (i + 1) * STRIP)
        rotated = jnp.dot(turned[rows], right[...], preferred_element_type=jnp.float32)
        one = 0.95 * first[rows, :].astype(jnp.float32) + 0.05 * rotated
        two = 0.95 * second[rows, :].astype(jnp.float32) + 0.05 * rotated * rotated
        first_new[rows, :] = one.astype(jnp.bfloat16)
        second_new[rows, :] = two.astype(jnp.bfloat16)
        ratio[rows, :] = (one / (jnp.sqrt(two) + 1e-08)).astype(jnp.bfloat16)
    stores = [
        pltpu.make_async_copy(first_new, first_new_hbm, sems.at[0]),
        pltpu.make_async_copy(second_new, second_new_hbm, sems.at[1]),
    ]
    for c in stores:
        c.start()
    back = jnp.dot(left[...], ratio[...], preferred_element_type=jnp.float32).astype(jnp.bfloat16)
    block_update = lax.dot_general(
        back, right[...], (((1,), (1,)), ((), ())), preferred_element_type=jnp.float32
    ).astype(jnp.bfloat16)
    for here, natural in places:
        leaving[here, :] = block_update[natural, :]
    for c in stores:
        c.wait()


def step(*operands):
    square = jax.ShapeDtypeStruct((SIDE, SIDE), jnp.bfloat16)
    return pl.pallas_call(
        step_kernel,
        out_shape=(square, square, square),
        in_specs=[vmem()] * 6,
        out_specs=(hbm(), hbm(), vmem()),
        scratch_shapes=[pltpu.VMEM((SIDE, SIDE), jnp.bfloat16)] * 4 + [pltpu.SemaphoreType.DMA((2,))],
        compiler_params=pltpu.CompilerParams(vmem_limit_bytes=24 * 1024 * 1024),
        cost_estimate=pl.CostEstimate(
            flops=8 * SIDE**3, bytes_accessed=18 * SIDE**2, transcendentals=2 * SIDE**2
        ),
        name="soap_step",
    )(*operands)


def exchange(pieces):
    return lax.all_to_all(pieces, "fsdp", 0, 0, axis_index_groups=[ORDER], tiled=True)


def sum_over_x(pair):
    chips = [[2 * chip_of(p) + core for p in range(N_X)] for core in range(2)]
    parts = lax.all_to_all(pair, "rep", 0, 0, axis_index_groups=chips, tiled=True)
    return jnp.sum(parts.astype(jnp.float32), axis=0).astype(jnp.bfloat16)


def local(partials, left_basis, right_basis, first_moment, second_moment, owners):
    n_rep = 2 * N_X
    rep = lax.axis_index("rep")
    core = lax.rem(rep, 2)
    owner_row = lax.dynamic_slice_in_dim(owners, rep, 1, 0)[0]
    places = natural_of(owner_row)
    left = left_basis[0, 0]
    right = right_basis[0, 0]

    own = partials[0]
    other = lax.ppermute(own, "rep", [(i, i ^ 1) for i in range(n_rep)])
    other, left_turned, places = lax.optimization_barrier((other, left.T, places))
    pair = add_pair(own, other)
    early = lax.cond(core == 1, sum_over_x, lambda p: jnp.zeros(p.shape[1:], p.dtype), pair)
    follow = lax.ppermute(early[0], "rep", [(i + 1, i) for i in range(0, n_rep, 2)])
    pair = add_pair(own, other, follow)
    pieces = lax.cond(core == 0, lambda p, e: sum_over_x(p), lambda p, e: e, pair, early)

    arrived = exchange(place_blocks(places, pieces))
    first_new, second_new, leaving = step(
        arrived.reshape(SIDE, SIDE), left, left_turned, right, first_moment[0, 0], second_moment[0, 0]
    )
    returned = exchange(leaving.reshape(N_FSDP, SUB, SIDE))
    update = pick_blocks(places, returned)
    return (first_new[None, None], second_new[None, None], update)


def solution(mesh):
    return jax.shard_map(
        local,
        mesh=mesh,
        in_specs=(
            P("rep", None, "fsdp", None),
            P("rep", "fsdp", None, None),
            P("rep", "fsdp", None, None),
            P("rep", "fsdp", None, None),
            P("rep", "fsdp", None, None),
            P(),
        ),
        out_specs=(
            P("rep", "fsdp", None, None),
            P("rep", "fsdp", None, None),
            P(None, "fsdp", "rep"),
        ),
        check_vma=False,
    )
```

```python
import jax
import jax.numpy as jnp
from jax import lax
from jax.experimental import pallas as pl
from jax.experimental.pallas import tpu as pltpu
from jax.sharding import PartitionSpec as P

N_X = 4
N_Y = 4
N_Z = 16
N_FSDP = N_Z * N_Y
SUB = 8
SIDE = 512
BLOCKS = 16
STRIP = 128

def natural_of(p):
    return (p // N_Y + N_Z // 2) % N_Z * N_Y + (p % N_Y + N_Y // 2) % N_Y


def chip_of(p):
    return (p + N_X // 2) % N_X


ORDER = [natural_of(p) for p in range(N_FSDP)]
PAIR = 2 * SUB


def hbm():
    return pl.BlockSpec(memory_space=pl.ANY)


def vmem():
    return pl.BlockSpec(memory_space=pltpu.VMEM)


def pair_kernel(own, other, *refs):
    pair = refs[-1]
    core = lax.rem(lax.axis_index("rep"), 2)
    for p in range(N_X):
        columns = pl.ds(pl.multiple_of((2 * chip_of(p) + core) * SIDE, SIDE), SIDE)
        total = own[:, :, columns].astype(jnp.float32) + other[:, :, columns].astype(jnp.float32)
        pair[p] = total.astype(jnp.bfloat16)


def add_pair(own, other, *after):
    return pl.pallas_call(
        pair_kernel,
        out_shape=jax.ShapeDtypeStruct((N_X, BLOCKS, SUB, SIDE), jnp.bfloat16),
        in_specs=[vmem(), vmem()] + [vmem()] * len(after),
        out_specs=vmem(),
        compiler_params=pltpu.CompilerParams(vmem_limit_bytes=16 * 1024 * 1024),
        name="add_pair",
    )(own, other, *after)


def place_kernel(places, pieces, outgoing):
    for b in range(BLOCKS):
        outgoing[places[b]] = pieces[b]


def place_blocks(places, pieces):
    return pl.pallas_call(
        place_kernel,
        out_shape=jax.ShapeDtypeStruct((N_FSDP, SUB, SIDE), jnp.bfloat16),
        in_specs=[pl.BlockSpec(memory_space=pltpu.SMEM), vmem()],
        out_specs=vmem(),
        compiler_params=pltpu.CompilerParams(vmem_limit_bytes=16 * 1024 * 1024),
        name="place_blocks",
    )(places, pieces)


def step_kernel(
    owned, arrived, left, left_turned, right, first, second,
    first_new_hbm, second_new_hbm, leaving,
    grad, first_new, second_new, ratio, sems,
):
    places = [
        (slice(p * SUB, p * SUB + PAIR), slice(ORDER[p] * SUB, ORDER[p] * SUB + PAIR))
        for p in range(0, N_FSDP, 2)
    ]
    for here, natural in places:
        grad[natural, :] = arrived[here, :]
    turned = jnp.dot(left_turned[...], grad[...], preferred_element_type=jnp.float32).astype(
        jnp.bfloat16
    )
    for i in range(SIDE // STRIP):
        rows = slice(i * STRIP, (i + 1) * STRIP)
        rotated = jnp.dot(turned[rows], right[...], preferred_element_type=jnp.float32)
        rotated = jnp.where(owned[0] == 1, rotated, 0.0)
        one = 0.95 * first[rows, :].astype(jnp.float32) + 0.05 * rotated
        two = 0.95 * second[rows, :].astype(jnp.float32) + 0.05 * rotated * rotated
        first_new[rows, :] = one.astype(jnp.bfloat16)
        second_new[rows, :] = two.astype(jnp.bfloat16)
        ratio[rows, :] = (one / (two * lax.rsqrt(two) + 1e-08)).astype(jnp.bfloat16)
    stores = [
        pltpu.make_async_copy(first_new, first_new_hbm, sems.at[0]),
        pltpu.make_async_copy(second_new, second_new_hbm, sems.at[1]),
    ]
    for c in stores:
        c.start()
    back = jnp.dot(left[...], ratio[...], preferred_element_type=jnp.float32).astype(jnp.bfloat16)
    block_update = lax.dot_general(
        back, right[...], (((1,), (1,)), ((), ())), preferred_element_type=jnp.float32
    ).astype(jnp.bfloat16)
    for here, natural in places:
        leaving[here, :] = block_update[natural, :]
    for c in stores:
        c.wait()


def step(*operands):
    square = jax.ShapeDtypeStruct((SIDE, SIDE), jnp.bfloat16)
    return pl.pallas_call(
        step_kernel,
        out_shape=(square, square, square),
        in_specs=[pl.BlockSpec(memory_space=pltpu.SMEM)] + [vmem()] * 6,
        out_specs=(hbm(), hbm(), vmem()),
        scratch_shapes=[pltpu.VMEM((SIDE, SIDE), jnp.bfloat16)] * 4 + [pltpu.SemaphoreType.DMA((2,))],
        compiler_params=pltpu.CompilerParams(vmem_limit_bytes=24 * 1024 * 1024),
        cost_estimate=pl.CostEstimate(
            flops=8 * SIDE**3, bytes_accessed=18 * SIDE**2, transcendentals=2 * SIDE**2
        ),
        name="soap_step",
    )(*operands)


def exchange(pieces):
    return lax.all_to_all(pieces, "fsdp", 0, 0, axis_index_groups=[ORDER], tiled=True)


def sum_over_x(pair):
    chips = [[2 * chip_of(p) + core for p in range(N_X)] for core in range(2)]
    parts = lax.all_to_all(pair, "rep", 0, 0, axis_index_groups=chips, tiled=True)
    return jnp.sum(parts.astype(jnp.float32), axis=0).astype(jnp.bfloat16)


def local(partials, left_basis, right_basis, first_moment, second_moment, owners):
    n_rep = 2 * N_X
    rep = lax.axis_index("rep")
    core = lax.rem(rep, 2)
    owner_row = lax.dynamic_slice_in_dim(owners, rep, 1, 0)[0]
    places = natural_of(owner_row)
    slots = jnp.arange(N_FSDP, dtype=jnp.int32)
    selector = (places[None, :] == slots[:, None]).astype(jnp.bfloat16)
    owned = jnp.any(owner_row == lax.axis_index("fsdp")).astype(jnp.int32).reshape(1)
    left = left_basis[0, 0]
    right = right_basis[0, 0]

    own = partials[0]
    other = lax.ppermute(own, "rep", [(i, i ^ 1) for i in range(n_rep)])
    other, left_turned, places, selector, owned = lax.optimization_barrier(
        (other, left.T, places, selector, owned)
    )
    pair = add_pair(own, other)
    early = lax.cond(core == 1, sum_over_x, lambda p: jnp.zeros(p.shape[1:], p.dtype), pair)
    follow = lax.ppermute(early[0], "rep", [(i + 1, i) for i in range(0, n_rep, 2)])
    pair = add_pair(own, other, follow)
    pieces = lax.cond(core == 0, lambda p, e: sum_over_x(p), lambda p, e: e, pair, early)

    arrived = exchange(place_blocks(places, pieces))
    first_new, second_new, leaving = step(
        owned, arrived.reshape(SIDE, SIDE), left, left_turned, right,
        first_moment[0, 0], second_moment[0, 0],
    )
    returned = exchange(leaving.reshape(N_FSDP, SUB, SIDE))
    update = jnp.einsum(
        "qb,qsk->bsk", selector, returned, preferred_element_type=jnp.float32
    ).astype(jnp.bfloat16)
    return (first_new[None, None], second_new[None, None], update)


def solution(mesh):
    return jax.shard_map(
        local,
        mesh=mesh,
        in_specs=(
            P("rep", None, "fsdp", None),
            P("rep", "fsdp", None, None),
            P("rep", "fsdp", None, None),
            P("rep", "fsdp", None, None),
            P("rep", "fsdp", None, None),
            P(),
        ),
        out_specs=(
            P("rep", "fsdp", None, None),
            P("rep", "fsdp", None, None),
            P(None, "fsdp", "rep"),
        ),
        check_vma=False,
    )
```

```python
import jax
import jax.numpy as jnp
from jax import lax
from jax.experimental import pallas as pl
from jax.experimental.pallas import tpu as pltpu
from jax.sharding import PartitionSpec as P

N_X = 4
N_Y = 4
N_Z = 16
N_FSDP = N_Z * N_Y
SUB = 8
SIDE = 512
BLOCKS = 16
STRIP = 128

def natural_of(p):
    return (p // N_Y + N_Z // 2) % N_Z * N_Y + (p % N_Y + N_Y // 2) % N_Y


def chip_of(p):
    return (p + N_X // 2) % N_X


ORDER = [natural_of(p) for p in range(N_FSDP)]
PAIR = 2 * SUB


def hbm():
    return pl.BlockSpec(memory_space=pl.ANY)


def vmem():
    return pl.BlockSpec(memory_space=pltpu.VMEM)


def pair_kernel(own, other, *refs):
    pair = refs[-1]
    core = lax.rem(lax.axis_index("rep"), 2)
    for p in range(N_X):
        columns = pl.ds(pl.multiple_of((2 * chip_of(p) + core) * SIDE, SIDE), SIDE)
        total = own[:, :, columns].astype(jnp.float32) + other[:, :, columns].astype(jnp.float32)
        pair[p] = total.astype(jnp.bfloat16)


def add_pair(own, other, *after):
    return pl.pallas_call(
        pair_kernel,
        out_shape=jax.ShapeDtypeStruct((N_X, BLOCKS, SUB, SIDE), jnp.bfloat16),
        in_specs=[vmem(), vmem()] + [vmem()] * len(after),
        out_specs=vmem(),
        compiler_params=pltpu.CompilerParams(vmem_limit_bytes=16 * 1024 * 1024),
        name="add_pair",
    )(own, other, *after)


def place_kernel(owners, pieces, outgoing):
    rep = lax.axis_index("rep")
    outgoing[...] = jnp.zeros_like(outgoing)
    for b in range(BLOCKS):
        outgoing[natural_of(owners[rep, b])] = pieces[b]


def place_blocks(owners, pieces):
    return pl.pallas_call(
        place_kernel,
        out_shape=jax.ShapeDtypeStruct((N_FSDP, SUB, SIDE), jnp.bfloat16),
        in_specs=[pl.BlockSpec(memory_space=pltpu.SMEM), vmem()],
        out_specs=vmem(),
        compiler_params=pltpu.CompilerParams(vmem_limit_bytes=16 * 1024 * 1024),
        name="place_blocks",
    )(owners, pieces)


def step_kernel(
    arrived, left, left_turned, right, first, second,
    first_new_hbm, second_new_hbm, leaving,
    grad, first_new, second_new, ratio, sems,
):
    places = [
        (slice(p * SUB, p * SUB + PAIR), slice(ORDER[p] * SUB, ORDER[p] * SUB + PAIR))
        for p in range(0, N_FSDP, 2)
    ]
    for here, natural in places:
        grad[natural, :] = arrived[here, :]
    turned = jnp.dot(left_turned[...], grad[...], preferred_element_type=jnp.float32).astype(
        jnp.bfloat16
    )
    for i in range(SIDE // STRIP):
        rows = slice(i * STRIP, (i + 1) * STRIP)
        rotated = jnp.dot(turned[rows], right[...], preferred_element_type=jnp.float32)
        one = 0.95 * first[rows, :].astype(jnp.float32) + 0.05 * rotated
        two = 0.95 * second[rows, :].astype(jnp.float32) + 0.05 * rotated * rotated
        first_new[rows, :] = one.astype(jnp.bfloat16)
        second_new[rows, :] = two.astype(jnp.bfloat16)
        ratio[rows, :] = (one / (two * lax.rsqrt(two) + 1e-08)).astype(jnp.bfloat16)
    stores = [
        pltpu.make_async_copy(first_new, first_new_hbm, sems.at[0]),
        pltpu.make_async_copy(second_new, second_new_hbm, sems.at[1]),
    ]
    for c in stores:
        c.start()
    back = jnp.dot(left[...], ratio[...], preferred_element_type=jnp.float32).astype(jnp.bfloat16)
    block_update = lax.dot_general(
        back, right[...], (((1,), (1,)), ((), ())), preferred_element_type=jnp.float32
    ).astype(jnp.bfloat16)
    for here, natural in places:
        leaving[here, :] = block_update[natural, :]
    for c in stores:
        c.wait()


def step(*operands):
    square = jax.ShapeDtypeStruct((SIDE, SIDE), jnp.bfloat16)
    return pl.pallas_call(
        step_kernel,
        out_shape=(square, square, square),
        in_specs=[vmem()] * 6,
        out_specs=(hbm(), hbm(), vmem()),
        scratch_shapes=[pltpu.VMEM((SIDE, SIDE), jnp.bfloat16)] * 4 + [pltpu.SemaphoreType.DMA((2,))],
        compiler_params=pltpu.CompilerParams(vmem_limit_bytes=24 * 1024 * 1024),
        cost_estimate=pl.CostEstimate(
            flops=8 * SIDE**3, bytes_accessed=18 * SIDE**2, transcendentals=2 * SIDE**2
        ),
        name="soap_step",
    )(*operands)


def exchange(pieces):
    return lax.all_to_all(pieces, "fsdp", 0, 0, axis_index_groups=[ORDER], tiled=True)


def sum_over_x(pair):
    chips = [[2 * chip_of(p) + core for p in range(N_X)] for core in range(2)]
    parts = lax.all_to_all(pair, "rep", 0, 0, axis_index_groups=chips, tiled=True)
    return jnp.sum(parts.astype(jnp.float32), axis=0).astype(jnp.bfloat16)


def local(partials, left_basis, right_basis, first_moment, second_moment, owners):
    n_rep = 2 * N_X
    rep = lax.axis_index("rep")
    core = lax.rem(rep, 2)
    owner_row = lax.dynamic_slice_in_dim(owners, rep, 1, 0)[0]
    slots = natural_of(jnp.arange(N_FSDP, dtype=jnp.int32))
    selector = (owner_row[None, :] == slots[:, None]).astype(jnp.bfloat16)
    left = left_basis[0, 0]
    right = right_basis[0, 0]

    own = partials[0]
    other = lax.ppermute(own, "rep", [(i, i ^ 1) for i in range(n_rep)])
    other, left_turned, selector = lax.optimization_barrier((other, left.T, selector))
    pair = add_pair(own, other)
    early = lax.cond(core == 1, sum_over_x, lambda p: jnp.zeros(p.shape[1:], p.dtype), pair)
    follow = lax.ppermute(early[0], "rep", [(i + 1, i) for i in range(0, n_rep, 2)])
    pair = add_pair(own, other, follow)
    pieces = lax.cond(core == 0, lambda p, e: sum_over_x(p), lambda p, e: e, pair, early)

    arrived = exchange(place_blocks(owners, pieces))
    first_new, second_new, leaving = step(
        arrived.reshape(SIDE, SIDE), left, left_turned, right,
        first_moment[0, 0], second_moment[0, 0],
    )
    returned = exchange(leaving.reshape(N_FSDP, SUB, SIDE))
    update = jnp.einsum(
        "qb,qsk->bsk", selector, returned, preferred_element_type=jnp.float32
    ).astype(jnp.bfloat16)
    return (first_new[None, None], second_new[None, None], update)


def solution(mesh):
    return jax.shard_map(
        local,
        mesh=mesh,
        in_specs=(
            P("rep", None, "fsdp", None),
            P("rep", "fsdp", None, None),
            P("rep", "fsdp", None, None),
            P("rep", "fsdp", None, None),
            P("rep", "fsdp", None, None),
            P(),
        ),
        out_specs=(
            P("rep", "fsdp", None, None),
            P("rep", "fsdp", None, None),
            P(None, "fsdp", "rep"),
        ),
        check_vma=False,
    )
```

```python
import jax
import jax.numpy as jnp
from jax import lax
from jax.experimental import pallas as pl
from jax.experimental.pallas import tpu as pltpu
from jax.sharding import PartitionSpec as P

N_X = 4
N_Y = 4
N_Z = 16
N_FSDP = N_Z * N_Y
SUB = 8
SIDE = 512
BLOCKS = 16
STRIP = 128

PLANES = [8, 0, 1, 15, 2, 14, 3, 13, 4, 12, 5, 11, 6, 10, 7, 9]
ORDER = [z * N_Y + (y + N_Y // 2) % N_Y for z in PLANES for y in range(N_Y)]
PAIR = 2 * SUB


def chip_of(p):
    return (p + N_X // 2) % N_X


def hbm():
    return pl.BlockSpec(memory_space=pl.ANY)


def vmem():
    return pl.BlockSpec(memory_space=pltpu.VMEM)


def pair_kernel(own, other, *refs):
    pair = refs[-1]
    core = lax.rem(lax.axis_index("rep"), 2)
    for p in range(N_X):
        columns = pl.ds(pl.multiple_of((2 * chip_of(p) + core) * SIDE, SIDE), SIDE)
        total = own[:, :, columns].astype(jnp.float32) + other[:, :, columns].astype(jnp.float32)
        pair[p] = total.astype(jnp.bfloat16)


def add_pair(own, other, *after):
    return pl.pallas_call(
        pair_kernel,
        out_shape=jax.ShapeDtypeStruct((N_X, BLOCKS, SUB, SIDE), jnp.bfloat16),
        in_specs=[vmem(), vmem()] + [vmem()] * len(after),
        out_specs=vmem(),
        compiler_params=pltpu.CompilerParams(vmem_limit_bytes=16 * 1024 * 1024),
        name="add_pair",
    )(own, other, *after)


def step_kernel(
    arrived, left, left_turned, right, first, second,
    first_new_hbm, second_new_hbm, leaving,
    grad, first_new, second_new, ratio, sems,
):
    places = [
        (slice(p * SUB, p * SUB + PAIR), slice(ORDER[p] * SUB, ORDER[p] * SUB + PAIR))
        for p in range(0, N_FSDP, 2)
    ]
    for here, natural in places:
        grad[natural, :] = arrived[here, :]
    turned = jnp.dot(left_turned[...], grad[...], preferred_element_type=jnp.float32).astype(
        jnp.bfloat16
    )
    for i in range(SIDE // STRIP):
        rows = slice(i * STRIP, (i + 1) * STRIP)
        rotated = jnp.dot(turned[rows], right[...], preferred_element_type=jnp.float32)
        one = 0.95 * first[rows, :].astype(jnp.float32) + 0.05 * rotated
        two = 0.95 * second[rows, :].astype(jnp.float32) + 0.05 * rotated * rotated
        first_new[rows, :] = one.astype(jnp.bfloat16)
        second_new[rows, :] = two.astype(jnp.bfloat16)
        ratio[rows, :] = (one / (two * lax.rsqrt(two) + 1e-08)).astype(jnp.bfloat16)
    stores = [
        pltpu.make_async_copy(first_new, first_new_hbm, sems.at[0]),
        pltpu.make_async_copy(second_new, second_new_hbm, sems.at[1]),
    ]
    for c in stores:
        c.start()
    back = jnp.dot(left[...], ratio[...], preferred_element_type=jnp.float32).astype(jnp.bfloat16)
    block_update = lax.dot_general(
        back, right[...], (((1,), (1,)), ((), ())), preferred_element_type=jnp.float32
    ).astype(jnp.bfloat16)
    for here, natural in places:
        leaving[here, :] = block_update[natural, :]
    for c in stores:
        c.wait()


def step(*operands):
    square = jax.ShapeDtypeStruct((SIDE, SIDE), jnp.bfloat16)
    return pl.pallas_call(
        step_kernel,
        out_shape=(square, square, square),
        in_specs=[vmem()] * 6,
        out_specs=(hbm(), hbm(), vmem()),
        scratch_shapes=[pltpu.VMEM((SIDE, SIDE), jnp.bfloat16)] * 4 + [pltpu.SemaphoreType.DMA((2,))],
        compiler_params=pltpu.CompilerParams(vmem_limit_bytes=24 * 1024 * 1024),
        cost_estimate=pl.CostEstimate(
            flops=8 * SIDE**3, bytes_accessed=18 * SIDE**2, transcendentals=2 * SIDE**2
        ),
        name="soap_step",
    )(*operands)


def exchange(pieces):
    return lax.all_to_all(pieces, "fsdp", 0, 0, axis_index_groups=[ORDER], tiled=True)


def sum_over_x(pair):
    chips = [[2 * chip_of(p) + core for p in range(N_X)] for core in range(2)]
    parts = lax.all_to_all(pair, "rep", 0, 0, axis_index_groups=chips, tiled=True)
    return jnp.sum(parts.astype(jnp.float32), axis=0).astype(jnp.bfloat16)


def local(partials, left_basis, right_basis, first_moment, second_moment, owners):
    n_rep = 2 * N_X
    rep = lax.axis_index("rep")
    core = lax.rem(rep, 2)
    owner_row = lax.dynamic_slice_in_dim(owners, rep, 1, 0)[0]
    slots = jnp.array(ORDER, jnp.int32)
    selector = (owner_row[None, :] == slots[:, None]).astype(jnp.bfloat16)
    left = left_basis[0, 0]
    right = right_basis[0, 0]

    own = partials[0]
    other = lax.ppermute(own, "rep", [(i, i ^ 1) for i in range(n_rep)])
    other, left_turned, selector = lax.optimization_barrier((other, left.T, selector))
    pair = add_pair(own, other)
    early = lax.cond(core == 1, sum_over_x, lambda p: jnp.zeros(p.shape[1:], p.dtype), pair)
    follow = lax.ppermute(early[0], "rep", [(i + 1, i) for i in range(0, n_rep, 2)])
    pair = add_pair(own, other, follow)
    pieces = lax.cond(core == 0, lambda p, e: sum_over_x(p), lambda p, e: e, pair, early)

    outgoing = jnp.einsum(
        "qb,bsk->qsk", selector, pieces, preferred_element_type=jnp.float32
    ).astype(jnp.bfloat16)
    arrived = exchange(outgoing)
    first_new, second_new, leaving = step(
        arrived.reshape(SIDE, SIDE), left, left_turned, right,
        first_moment[0, 0], second_moment[0, 0],
    )
    returned = exchange(leaving.reshape(N_FSDP, SUB, SIDE))
    update = jnp.einsum(
        "qb,qsk->bsk", selector, returned, preferred_element_type=jnp.float32
    ).astype(jnp.bfloat16)
    return (first_new[None, None], second_new[None, None], update)


def solution(mesh):
    return jax.shard_map(
        local,
        mesh=mesh,
        in_specs=(
            P("rep", None, "fsdp", None),
            P("rep", "fsdp", None, None),
            P("rep", "fsdp", None, None),
            P("rep", "fsdp", None, None),
            P("rep", "fsdp", None, None),
            P(),
        ),
        out_specs=(
            P("rep", "fsdp", None, None),
            P("rep", "fsdp", None, None),
            P(None, "fsdp", "rep"),
        ),
        check_vma=False,
    )
```

```python
import jax
import jax.numpy as jnp
from jax import lax
from jax.experimental import pallas as pl
from jax.experimental.pallas import tpu as pltpu
from jax.sharding import PartitionSpec as P

N_X = 4
N_Y = 4
N_Z = 16
N_FSDP = N_Z * N_Y
SUB = 8
SIDE = 512
BLOCKS = 16
STRIP = 256

def natural_of(p):
    return (p // N_Y + N_Z // 2) % N_Z * N_Y + (p % N_Y + N_Y // 2) % N_Y


def chip_of(p):
    return (p + N_X // 2) % N_X


ORDER = [natural_of(p) for p in range(N_FSDP)]
PAIR = 2 * SUB


def hbm():
    return pl.BlockSpec(memory_space=pl.ANY)


def vmem():
    return pl.BlockSpec(memory_space=pltpu.VMEM)


def pair_kernel(own, other, *refs):
    pair = refs[-1]
    core = lax.rem(lax.axis_index("rep"), 2)
    for p in range(N_X):
        columns = pl.ds(pl.multiple_of((2 * chip_of(p) + core) * SIDE, SIDE), SIDE)
        total = own[:, :, columns].astype(jnp.float32) + other[:, :, columns].astype(jnp.float32)
        pair[p] = total.astype(jnp.bfloat16)


def add_pair(own, other, *after):
    return pl.pallas_call(
        pair_kernel,
        out_shape=jax.ShapeDtypeStruct((N_X, BLOCKS, SUB, SIDE), jnp.bfloat16),
        in_specs=[vmem(), vmem()] + [vmem()] * len(after),
        out_specs=vmem(),
        compiler_params=pltpu.CompilerParams(vmem_limit_bytes=16 * 1024 * 1024),
        name="add_pair",
    )(own, other, *after)


def step_kernel(
    arrived, left, left_turned, right, first, second,
    first_new_hbm, second_new_hbm, leaving,
    grad, first_new, second_new, sems,
):
    places = [
        (slice(p * SUB, p * SUB + PAIR), slice(ORDER[p] * SUB, ORDER[p] * SUB + PAIR))
        for p in range(0, N_FSDP, 2)
    ]
    for here, natural in places:
        grad[natural, :] = arrived[here, :]
    strips = [slice(i, i + STRIP) for i in range(0, SIDE, STRIP)]
    total = None
    for rows in strips:
        turned = jnp.dot(
            left_turned[rows, :], grad[...], preferred_element_type=jnp.float32
        ).astype(jnp.bfloat16)
        rotated = jnp.dot(turned, right[...], preferred_element_type=jnp.float32)
        one = 0.95 * first[rows, :].astype(jnp.float32) + 0.05 * rotated
        two = 0.95 * second[rows, :].astype(jnp.float32) + 0.05 * rotated * rotated
        first_new[rows, :] = one.astype(jnp.bfloat16)
        second_new[rows, :] = two.astype(jnp.bfloat16)
        ratio = (one / (two * lax.rsqrt(two) + 1e-08)).astype(jnp.bfloat16)
        part = jnp.dot(left[:, rows], ratio, preferred_element_type=jnp.float32)
        total = part if total is None else total + part
    stores = [
        pltpu.make_async_copy(first_new, first_new_hbm, sems.at[0]),
        pltpu.make_async_copy(second_new, second_new_hbm, sems.at[1]),
    ]
    for c in stores:
        c.start()
    back = total.astype(jnp.bfloat16)
    block_update = lax.dot_general(
        back, right[...], (((1,), (1,)), ((), ())), preferred_element_type=jnp.float32
    ).astype(jnp.bfloat16)
    for here, natural in places:
        leaving[here, :] = block_update[natural, :]
    for c in stores:
        c.wait()


def step(*operands):
    square = jax.ShapeDtypeStruct((SIDE, SIDE), jnp.bfloat16)
    return pl.pallas_call(
        step_kernel,
        out_shape=(square, square, square),
        in_specs=[vmem()] * 6,
        out_specs=(hbm(), hbm(), vmem()),
        scratch_shapes=[pltpu.VMEM((SIDE, SIDE), jnp.bfloat16)] * 3 + [pltpu.SemaphoreType.DMA((2,))],
        compiler_params=pltpu.CompilerParams(vmem_limit_bytes=24 * 1024 * 1024),
        cost_estimate=pl.CostEstimate(
            flops=8 * SIDE**3, bytes_accessed=18 * SIDE**2, transcendentals=2 * SIDE**2
        ),
        name="soap_step",
    )(*operands)


def exchange(pieces):
    return lax.all_to_all(pieces, "fsdp", 0, 0, axis_index_groups=[ORDER], tiled=True)


def sum_over_x(pair):
    chips = [[2 * chip_of(p) + core for p in range(N_X)] for core in range(2)]
    parts = lax.all_to_all(pair, "rep", 0, 0, axis_index_groups=chips, tiled=True)
    return jnp.sum(parts.astype(jnp.float32), axis=0).astype(jnp.bfloat16)


def local(partials, left_basis, right_basis, first_moment, second_moment, owners):
    n_rep = 2 * N_X
    rep = lax.axis_index("rep")
    core = lax.rem(rep, 2)
    owner_row = lax.dynamic_slice_in_dim(owners, rep, 1, 0)[0]
    slots = natural_of(jnp.arange(N_FSDP, dtype=jnp.int32))
    selector = (owner_row[None, :] == slots[:, None]).astype(jnp.bfloat16)
    left = left_basis[0, 0]
    right = right_basis[0, 0]

    own = partials[0]
    other = lax.ppermute(own, "rep", [(i, i ^ 1) for i in range(n_rep)])
    other, left_turned, selector = lax.optimization_barrier((other, left.T, selector))
    pair = add_pair(own, other)
    early = lax.cond(core == 1, sum_over_x, lambda p: jnp.zeros(p.shape[1:], p.dtype), pair)
    follow = lax.ppermute(early[0], "rep", [(i + 1, i) for i in range(0, n_rep, 2)])
    pair = add_pair(own, other, follow)
    pieces = lax.cond(core == 0, lambda p, e: sum_over_x(p), lambda p, e: e, pair, early)

    outgoing = jnp.einsum(
        "qb,bsk->qsk", selector, pieces, preferred_element_type=jnp.float32
    ).astype(jnp.bfloat16)
    arrived = exchange(outgoing)
    first_new, second_new, leaving = step(
        arrived.reshape(SIDE, SIDE), left, left_turned, right,
        first_moment[0, 0], second_moment[0, 0],
    )
    returned = exchange(leaving.reshape(N_FSDP, SUB, SIDE))
    update = jnp.einsum(
        "qb,qsk->bsk", selector, returned, preferred_element_type=jnp.float32
    ).astype(jnp.bfloat16)
    return (first_new[None, None], second_new[None, None], update)


def solution(mesh):
    return jax.shard_map(
        local,
        mesh=mesh,
        in_specs=(
            P("rep", None, "fsdp", None),
            P("rep", "fsdp", None, None),
            P("rep", "fsdp", None, None),
            P("rep", "fsdp", None, None),
            P("rep", "fsdp", None, None),
            P(),
        ),
        out_specs=(
            P("rep", "fsdp", None, None),
            P("rep", "fsdp", None, None),
            P(None, "fsdp", "rep"),
        ),
        check_vma=False,
    )
```

```python
import jax
import jax.numpy as jnp
from jax import lax
from jax.experimental import pallas as pl
from jax.experimental.pallas import tpu as pltpu
from jax.sharding import PartitionSpec as P

N_X = 4
N_Y = 4
N_Z = 16
N_FSDP = N_Z * N_Y
SUB = 8
SIDE = 512
BLOCKS = 16
STRIP = 256

def natural_of(p):
    return (p // N_Y + N_Z // 2) % N_Z * N_Y + (p % N_Y + N_Y // 2) % N_Y


def chip_of(p):
    return (p + N_X // 2) % N_X


ORDER = [natural_of(p) for p in range(N_FSDP)]
PAIR = 2 * SUB


def hbm():
    return pl.BlockSpec(memory_space=pl.ANY)


def vmem():
    return pl.BlockSpec(memory_space=pltpu.VMEM)


def pair_kernel(own, other, *refs):
    pair = refs[-1]
    core = lax.rem(lax.axis_index("rep"), 2)
    for p in range(N_X):
        columns = pl.ds(pl.multiple_of((2 * chip_of(p) + core) * SIDE, SIDE), SIDE)
        total = own[:, :, columns].astype(jnp.float32) + other[:, :, columns].astype(jnp.float32)
        pair[p] = total.astype(jnp.bfloat16)


def add_pair(own, other, *after):
    return pl.pallas_call(
        pair_kernel,
        out_shape=jax.ShapeDtypeStruct((N_X, BLOCKS, SUB, SIDE), jnp.bfloat16),
        in_specs=[vmem(), vmem()] + [vmem()] * len(after),
        out_specs=vmem(),
        compiler_params=pltpu.CompilerParams(vmem_limit_bytes=16 * 1024 * 1024),
        name="add_pair",
    )(own, other, *after)


def step_kernel(
    arrived, left, left_turned, right, first, second,
    first_new_hbm, second_new_hbm, leaving,
    grad, first_new, second_new, sems,
):
    places = [
        (slice(p * SUB, p * SUB + PAIR), slice(ORDER[p] * SUB, ORDER[p] * SUB + PAIR))
        for p in range(0, N_FSDP, 2)
    ]
    for here, natural in places:
        grad[natural, :] = arrived[here, :]
    strips = [slice(i, i + STRIP) for i in range(0, SIDE, STRIP)]
    total = None
    for rows in strips:
        turned = jnp.dot(
            left_turned[rows, :], grad[...], preferred_element_type=jnp.float32
        ).astype(jnp.bfloat16)
        rotated = jnp.dot(turned, right[...], preferred_element_type=jnp.float32)
        one = 0.95 * first[rows, :].astype(jnp.float32) + 0.05 * rotated
        two = 0.95 * second[rows, :].astype(jnp.float32) + 0.05 * rotated * rotated
        first_new[rows, :] = one.astype(jnp.bfloat16)
        second_new[rows, :] = two.astype(jnp.bfloat16)
        ratio = (one / (two * lax.rsqrt(two) + 1e-08)).astype(jnp.bfloat16)
        part = jnp.dot(left[:, rows], ratio, preferred_element_type=jnp.float32)
        total = part if total is None else total + part
    stores = [
        pltpu.make_async_copy(first_new, first_new_hbm, sems.at[0]),
        pltpu.make_async_copy(second_new, second_new_hbm, sems.at[1]),
    ]
    for c in stores:
        c.start()
    back = total.astype(jnp.bfloat16)
    block_update = lax.dot_general(
        back, right[...], (((1,), (1,)), ((), ())), preferred_element_type=jnp.float32
    ).astype(jnp.bfloat16)
    for here, natural in places:
        leaving[here, :] = block_update[natural, :]
    for c in stores:
        c.wait()


def step(*operands):
    square = jax.ShapeDtypeStruct((SIDE, SIDE), jnp.bfloat16)
    return pl.pallas_call(
        step_kernel,
        out_shape=(square, square, square),
        in_specs=[vmem()] * 6,
        out_specs=(hbm(), hbm(), vmem()),
        scratch_shapes=[pltpu.VMEM((SIDE, SIDE), jnp.bfloat16)] * 3 + [pltpu.SemaphoreType.DMA((2,))],
        compiler_params=pltpu.CompilerParams(vmem_limit_bytes=24 * 1024 * 1024),
        cost_estimate=pl.CostEstimate(
            flops=8 * SIDE**3, bytes_accessed=18 * SIDE**2, transcendentals=2 * SIDE**2
        ),
        name="soap_step",
    )(*operands)


def exchange(pieces):
    return lax.all_to_all(pieces, "fsdp", 0, 0, axis_index_groups=[ORDER], tiled=True)


def sum_over_x(pair):
    chips = [[2 * chip_of(p) + core for p in range(N_X)] for core in range(2)]
    parts = lax.all_to_all(pair, "rep", 0, 0, axis_index_groups=chips, tiled=True)
    return jnp.sum(parts.astype(jnp.float32), axis=0).astype(jnp.bfloat16)


def to_owners(pieces, selector):
    outgoing = jnp.einsum(
        "qb,bsk->qsk", selector, pieces, preferred_element_type=jnp.float32
    ).astype(jnp.bfloat16)
    return exchange(outgoing)


def local(partials, left_basis, right_basis, first_moment, second_moment, owners):
    n_rep = 2 * N_X
    rep = lax.axis_index("rep")
    core = lax.rem(rep, 2)
    owner_row = lax.dynamic_slice_in_dim(owners, rep, 1, 0)[0]
    slots = natural_of(jnp.arange(N_FSDP, dtype=jnp.int32))
    selector = (owner_row[None, :] == slots[:, None]).astype(jnp.bfloat16)
    left = left_basis[0, 0]
    right = right_basis[0, 0]

    own = partials[0]
    other = lax.ppermute(own, "rep", [(i, i ^ 1) for i in range(n_rep)])
    other, left_turned, selector = lax.optimization_barrier((other, left.T, selector))
    pair = add_pair(own, other)
    early = lax.cond(core == 1, sum_over_x, lambda p: jnp.zeros(p.shape[1:], p.dtype), pair)
    follow = lax.ppermute(early[0], "rep", [(i + 1, i) for i in range(0, n_rep, 2)])
    arrived = lax.cond(
        core == 1, to_owners, lambda e, s: jnp.zeros((N_FSDP, SUB, SIDE), e.dtype), early, selector
    )
    pair = add_pair(own, other, follow)
    arrived = lax.cond(
        core == 0, lambda p, s, a: to_owners(sum_over_x(p), s), lambda p, s, a: a, pair, selector, arrived
    )
    first_new, second_new, leaving = step(
        arrived.reshape(SIDE, SIDE), left, left_turned, right,
        first_moment[0, 0], second_moment[0, 0],
    )
    returned = exchange(leaving.reshape(N_FSDP, SUB, SIDE))
    update = jnp.einsum(
        "qb,qsk->bsk", selector, returned, preferred_element_type=jnp.float32
    ).astype(jnp.bfloat16)
    return (first_new[None, None], second_new[None, None], update)


def solution(mesh):
    return jax.shard_map(
        local,
        mesh=mesh,
        in_specs=(
            P("rep", None, "fsdp", None),
            P("rep", "fsdp", None, None),
            P("rep", "fsdp", None, None),
            P("rep", "fsdp", None, None),
            P("rep", "fsdp", None, None),
            P(),
        ),
        out_specs=(
            P("rep", "fsdp", None, None),
            P("rep", "fsdp", None, None),
            P(None, "fsdp", "rep"),
        ),
        check_vma=False,
    )
```

```python
import jax
import jax.numpy as jnp
from jax import lax
from jax.experimental import pallas as pl
from jax.experimental.pallas import tpu as pltpu
from jax.sharding import PartitionSpec as P

N_X = 4
N_Y = 4
N_Z = 16
N_FSDP = N_Z * N_Y
SUB = 8
SIDE = 512
BLOCKS = 16
STRIP = 128

def natural_of(p):
    return (p // N_Y + N_Z // 2) % N_Z * N_Y + (p % N_Y + N_Y // 2) % N_Y


def chip_of(p):
    return (p + N_X // 2) % N_X


ORDER = [natural_of(p) for p in range(N_FSDP)]
PAIR = 2 * SUB


def hbm():
    return pl.BlockSpec(memory_space=pl.ANY)


def vmem():
    return pl.BlockSpec(memory_space=pltpu.VMEM)


def pair_kernel(own, other, *refs):
    pair = refs[-1]
    core = lax.rem(lax.axis_index("rep"), 2)
    for p in range(N_X):
        columns = pl.ds(pl.multiple_of((2 * chip_of(p) + core) * SIDE, SIDE), SIDE)
        total = own[:, :, columns].astype(jnp.float32) + other[:, :, columns].astype(jnp.float32)
        pair[p] = total.astype(jnp.bfloat16)


def add_pair(own, other, *after):
    return pl.pallas_call(
        pair_kernel,
        out_shape=jax.ShapeDtypeStruct((N_X, BLOCKS, SUB, SIDE), jnp.bfloat16),
        in_specs=[vmem(), vmem()] + [vmem()] * len(after),
        out_specs=vmem(),
        compiler_params=pltpu.CompilerParams(vmem_limit_bytes=16 * 1024 * 1024),
        name="add_pair",
    )(own, other, *after)


def step_kernel(
    arrived, left, left_turned, right, first, second,
    first_new_hbm, second_new_hbm, leaving,
    grad, first_new, second_new, ratio, sems,
):
    places = [
        (slice(p * SUB, p * SUB + PAIR), slice(ORDER[p] * SUB, ORDER[p] * SUB + PAIR))
        for p in range(0, N_FSDP, 2)
    ]
    for here, natural in places:
        grad[natural, :] = arrived[here, :]
    turned = jnp.dot(left_turned[...], grad[...], preferred_element_type=jnp.float32).astype(
        jnp.bfloat16
    )
    stores = []
    for i in range(SIDE // STRIP):
        rows = slice(i * STRIP, (i + 1) * STRIP)
        rotated = jnp.dot(turned[rows], right[...], preferred_element_type=jnp.float32)
        one = 0.95 * first[rows, :].astype(jnp.float32) + 0.05 * rotated
        two = 0.95 * second[rows, :].astype(jnp.float32) + 0.05 * rotated * rotated
        first_new[rows, :] = one.astype(jnp.bfloat16)
        second_new[rows, :] = two.astype(jnp.bfloat16)
        ratio[rows, :] = (one / (two * lax.rsqrt(two) + 1e-08)).astype(jnp.bfloat16)
        for j, (src, dst) in enumerate(((first_new, first_new_hbm), (second_new, second_new_hbm))):
            part = pl.ds(i * STRIP, STRIP)
            stores.append(pltpu.make_async_copy(src.at[part], dst.at[part], sems.at[2 * i + j]))
            stores[-1].start()
    back = jnp.dot(left[...], ratio[...], preferred_element_type=jnp.float32).astype(jnp.bfloat16)
    block_update = lax.dot_general(
        back, right[...], (((1,), (1,)), ((), ())), preferred_element_type=jnp.float32
    ).astype(jnp.bfloat16)
    for here, natural in places:
        leaving[here, :] = block_update[natural, :]
    for c in stores:
        c.wait()


def step(*operands):
    square = jax.ShapeDtypeStruct((SIDE, SIDE), jnp.bfloat16)
    return pl.pallas_call(
        step_kernel,
        out_shape=(square, square, square),
        in_specs=[vmem()] * 6,
        out_specs=(hbm(), hbm(), vmem()),
        scratch_shapes=[pltpu.VMEM((SIDE, SIDE), jnp.bfloat16)] * 4
        + [pltpu.SemaphoreType.DMA((2 * SIDE // STRIP,))],
        compiler_params=pltpu.CompilerParams(vmem_limit_bytes=24 * 1024 * 1024),
        cost_estimate=pl.CostEstimate(
            flops=8 * SIDE**3, bytes_accessed=18 * SIDE**2, transcendentals=2 * SIDE**2
        ),
        name="soap_step",
    )(*operands)


def exchange(pieces):
    return lax.all_to_all(pieces, "fsdp", 0, 0, axis_index_groups=[ORDER], tiled=True)


def sum_over_x(pair):
    chips = [[2 * chip_of(p) + core for p in range(N_X)] for core in range(2)]
    parts = lax.all_to_all(pair, "rep", 0, 0, axis_index_groups=chips, tiled=True)
    return jnp.sum(parts.astype(jnp.float32), axis=0).astype(jnp.bfloat16)


def local(partials, left_basis, right_basis, first_moment, second_moment, owners):
    n_rep = 2 * N_X
    rep = lax.axis_index("rep")
    core = lax.rem(rep, 2)
    owner_row = lax.dynamic_slice_in_dim(owners, rep, 1, 0)[0]
    slots = natural_of(jnp.arange(N_FSDP, dtype=jnp.int32))
    selector = (owner_row[None, :] == slots[:, None]).astype(jnp.bfloat16)
    left = left_basis[0, 0]
    right = right_basis[0, 0]

    own = partials[0]
    other = lax.ppermute(own, "rep", [(i, i ^ 1) for i in range(n_rep)])
    other, left_turned, selector = lax.optimization_barrier((other, left.T, selector))
    pair = add_pair(own, other)
    early = lax.cond(core == 1, sum_over_x, lambda p: jnp.zeros(p.shape[1:], p.dtype), pair)
    follow = lax.ppermute(early[0], "rep", [(i + 1, i) for i in range(0, n_rep, 2)])
    pair = add_pair(own, other, follow)
    pieces = lax.cond(core == 0, lambda p, e: sum_over_x(p), lambda p, e: e, pair, early)

    outgoing = jnp.einsum(
        "qb,bsk->qsk", selector, pieces, preferred_element_type=jnp.float32
    ).astype(jnp.bfloat16)
    arrived = exchange(outgoing)
    first_new, second_new, leaving = step(
        arrived.reshape(SIDE, SIDE), left, left_turned, right,
        first_moment[0, 0], second_moment[0, 0],
    )
    returned = exchange(leaving.reshape(N_FSDP, SUB, SIDE))
    update = jnp.einsum(
        "qb,qsk->bsk", selector, returned, preferred_element_type=jnp.float32
    ).astype(jnp.bfloat16)
    return (first_new[None, None], second_new[None, None], update)


def solution(mesh):
    return jax.shard_map(
        local,
        mesh=mesh,
        in_specs=(
            P("rep", None, "fsdp", None),
            P("rep", "fsdp", None, None),
            P("rep", "fsdp", None, None),
            P("rep", "fsdp", None, None),
            P("rep", "fsdp", None, None),
            P(),
        ),
        out_specs=(
            P("rep", "fsdp", None, None),
            P("rep", "fsdp", None, None),
            P(None, "fsdp", "rep"),
        ),
        check_vma=False,
    )
```

```python
import jax
import jax.numpy as jnp
from jax import lax
from jax.experimental import pallas as pl
from jax.experimental.pallas import tpu as pltpu
from jax.sharding import PartitionSpec as P

N_X = 4
N_Y = 4
N_Z = 16
LAST_Z = 10
N_FSDP = N_Z * N_Y
SUB = 8
SIDE = 512
BLOCKS = 16
STRIP = 128

def natural_of(p):
    return (p // N_Y + LAST_Z) % N_Z * N_Y + (p % N_Y + N_Y // 2) % N_Y


def chip_of(p):
    return (p + N_X // 2) % N_X


ORDER = [natural_of(p) for p in range(N_FSDP)]
PAIR = 2 * SUB


def hbm():
    return pl.BlockSpec(memory_space=pl.ANY)


def vmem():
    return pl.BlockSpec(memory_space=pltpu.VMEM)


def pair_kernel(own, other, *refs):
    pair = refs[-1]
    core = lax.rem(lax.axis_index("rep"), 2)
    for p in range(N_X):
        columns = pl.ds(pl.multiple_of((2 * chip_of(p) + core) * SIDE, SIDE), SIDE)
        total = own[:, :, columns].astype(jnp.float32) + other[:, :, columns].astype(jnp.float32)
        pair[p] = total.astype(jnp.bfloat16)


def add_pair(own, other, *after):
    return pl.pallas_call(
        pair_kernel,
        out_shape=jax.ShapeDtypeStruct((N_X, BLOCKS, SUB, SIDE), jnp.bfloat16),
        in_specs=[vmem(), vmem()] + [vmem()] * len(after),
        out_specs=vmem(),
        compiler_params=pltpu.CompilerParams(vmem_limit_bytes=16 * 1024 * 1024),
        name="add_pair",
    )(own, other, *after)


def step_kernel(
    arrived, left, left_turned, right, first, second,
    first_new_hbm, second_new_hbm, leaving,
    grad, first_new, second_new, ratio, sems,
):
    places = [
        (slice(p * SUB, p * SUB + PAIR), slice(ORDER[p] * SUB, ORDER[p] * SUB + PAIR))
        for p in range(0, N_FSDP, 2)
    ]
    for here, natural in places:
        grad[natural, :] = arrived[here, :]
    turned = jnp.dot(left_turned[...], grad[...], preferred_element_type=jnp.float32).astype(
        jnp.bfloat16
    )
    stores = []
    for i in range(SIDE // STRIP):
        rows = slice(i * STRIP, (i + 1) * STRIP)
        rotated = jnp.dot(turned[rows], right[...], preferred_element_type=jnp.float32)
        one = 0.95 * first[rows, :].astype(jnp.float32) + 0.05 * rotated
        two = 0.95 * second[rows, :].astype(jnp.float32) + 0.05 * rotated * rotated
        first_new[rows, :] = one.astype(jnp.bfloat16)
        second_new[rows, :] = two.astype(jnp.bfloat16)
        ratio[rows, :] = (one / (two * lax.rsqrt(two) + 1e-08)).astype(jnp.bfloat16)
        for j, (src, dst) in enumerate(((first_new, first_new_hbm), (second_new, second_new_hbm))):
            part = pl.ds(i * STRIP, STRIP)
            stores.append(pltpu.make_async_copy(src.at[part], dst.at[part], sems.at[2 * i + j]))
            stores[-1].start()
    back = jnp.dot(left[...], ratio[...], preferred_element_type=jnp.float32).astype(jnp.bfloat16)
    block_update = lax.dot_general(
        back, right[...], (((1,), (1,)), ((), ())), preferred_element_type=jnp.float32
    ).astype(jnp.bfloat16)
    for here, natural in places:
        leaving[here, :] = block_update[natural, :]
    for c in stores:
        c.wait()


def step(*operands):
    square = jax.ShapeDtypeStruct((SIDE, SIDE), jnp.bfloat16)
    return pl.pallas_call(
        step_kernel,
        out_shape=(square, square, square),
        in_specs=[vmem()] * 6,
        out_specs=(hbm(), hbm(), vmem()),
        scratch_shapes=[pltpu.VMEM((SIDE, SIDE), jnp.bfloat16)] * 4
        + [pltpu.SemaphoreType.DMA((2 * SIDE // STRIP,))],
        compiler_params=pltpu.CompilerParams(vmem_limit_bytes=24 * 1024 * 1024),
        cost_estimate=pl.CostEstimate(
            flops=8 * SIDE**3, bytes_accessed=18 * SIDE**2, transcendentals=2 * SIDE**2
        ),
        name="soap_step",
    )(*operands)


def exchange(pieces):
    return lax.all_to_all(pieces, "fsdp", 0, 0, axis_index_groups=[ORDER], tiled=True)


def sum_over_x(pair):
    chips = [[2 * chip_of(p) + core for p in range(N_X)] for core in range(2)]
    parts = lax.all_to_all(pair, "rep", 0, 0, axis_index_groups=chips, tiled=True)
    return jnp.sum(parts.astype(jnp.float32), axis=0).astype(jnp.bfloat16)


def local(partials, left_basis, right_basis, first_moment, second_moment, owners):
    n_rep = 2 * N_X
    rep = lax.axis_index("rep")
    core = lax.rem(rep, 2)
    owner_row = lax.dynamic_slice_in_dim(owners, rep, 1, 0)[0]
    slots = natural_of(jnp.arange(N_FSDP, dtype=jnp.int32))
    selector = (owner_row[None, :] == slots[:, None]).astype(jnp.bfloat16)
    left = left_basis[0, 0]
    right = right_basis[0, 0]

    own = partials[0]
    other = lax.ppermute(own, "rep", [(i, i ^ 1) for i in range(n_rep)])
    other, left_turned, selector = lax.optimization_barrier((other, left.T, selector))
    pair = add_pair(own, other)
    early = lax.cond(core == 1, sum_over_x, lambda p: jnp.zeros(p.shape[1:], p.dtype), pair)
    follow = lax.ppermute(early[0], "rep", [(i + 1, i) for i in range(0, n_rep, 2)])
    pair = add_pair(own, other, follow)
    pieces = lax.cond(core == 0, lambda p, e: sum_over_x(p), lambda p, e: e, pair, early)

    outgoing = jnp.einsum(
        "qb,bsk->qsk", selector, pieces, preferred_element_type=jnp.float32
    ).astype(jnp.bfloat16)
    arrived = exchange(outgoing)
    first_new, second_new, leaving = step(
        arrived.reshape(SIDE, SIDE), left, left_turned, right,
        first_moment[0, 0], second_moment[0, 0],
    )
    returned = exchange(leaving.reshape(N_FSDP, SUB, SIDE))
    update = jnp.einsum(
        "qb,qsk->bsk", selector, returned, preferred_element_type=jnp.float32
    ).astype(jnp.bfloat16)
    return (first_new[None, None], second_new[None, None], update)


def solution(mesh):
    return jax.shard_map(
        local,
        mesh=mesh,
        in_specs=(
            P("rep", None, "fsdp", None),
            P("rep", "fsdp", None, None),
            P("rep", "fsdp", None, None),
            P("rep", "fsdp", None, None),
            P("rep", "fsdp", None, None),
            P(),
        ),
        out_specs=(
            P("rep", "fsdp", None, None),
            P("rep", "fsdp", None, None),
            P(None, "fsdp", "rep"),
        ),
        check_vma=False,
    )
```

```python
import jax
import jax.numpy as jnp
from jax import lax
from jax.experimental import pallas as pl
from jax.experimental.pallas import tpu as pltpu
from jax.sharding import PartitionSpec as P

N_X = 4
N_Y = 4
N_Z = 16
N_FSDP = N_Z * N_Y
SUB = 8
SIDE = 512
BLOCKS = 16
STRIP = 128

def natural_of(p):
    return (p // N_Y + N_Z // 2) % N_Z * N_Y + (p % N_Y + N_Y // 2) % N_Y


def chip_of(p):
    return (p + N_X // 2) % N_X


ORDER = [natural_of(p) for p in range(N_FSDP)]
PAIR = 2 * SUB


def hbm():
    return pl.BlockSpec(memory_space=pl.ANY)


def vmem():
    return pl.BlockSpec(memory_space=pltpu.VMEM)


def pair_kernel(own, other, *refs):
    pair = refs[-1]
    core = lax.rem(lax.axis_index("rep"), 2)
    for p in range(N_X):
        columns = pl.ds(pl.multiple_of((2 * chip_of(p) + core) * SIDE, SIDE), SIDE)
        total = own[:, :, columns].astype(jnp.float32) + other[:, :, columns].astype(jnp.float32)
        pair[p] = total.astype(jnp.bfloat16)


def add_pair(own, other, *after):
    return pl.pallas_call(
        pair_kernel,
        out_shape=jax.ShapeDtypeStruct((N_X, BLOCKS, SUB, SIDE), jnp.bfloat16),
        in_specs=[vmem(), vmem()] + [vmem()] * len(after),
        out_specs=vmem(),
        compiler_params=pltpu.CompilerParams(vmem_limit_bytes=16 * 1024 * 1024),
        name="add_pair",
    )(own, other, *after)


def step_kernel(
    arrived, left, left_turned, right, first, second,
    first_new_hbm, second_new_hbm, leaving,
    grad, first_new, second_new, ratio, sems,
):
    places = [
        (slice(p * SUB, p * SUB + PAIR), slice(ORDER[p] * SUB, ORDER[p] * SUB + PAIR))
        for p in range(0, N_FSDP, 2)
    ]
    for here, natural in places:
        grad[natural, :] = arrived[here, :]
    turned = jnp.dot(left_turned[...], grad[...], preferred_element_type=jnp.float32).astype(
        jnp.bfloat16
    )
    stores = []
    for i in range(SIDE // STRIP):
        rows = slice(i * STRIP, (i + 1) * STRIP)
        rotated = jnp.dot(turned[rows], right[...], preferred_element_type=jnp.float32)
        one = 0.95 * first[rows, :].astype(jnp.float32) + 0.05 * rotated
        two = 0.95 * second[rows, :].astype(jnp.float32) + 0.05 * rotated * rotated
        first_new[rows, :] = one.astype(jnp.bfloat16)
        second_new[rows, :] = two.astype(jnp.bfloat16)
        ratio[rows, :] = (one / (two * lax.rsqrt(two) + 1e-08)).astype(jnp.bfloat16)
        for j, (src, dst) in enumerate(((first_new, first_new_hbm), (second_new, second_new_hbm))):
            part = pl.ds(i * STRIP, STRIP)
            stores.append(pltpu.make_async_copy(src.at[part], dst.at[part], sems.at[2 * i + j]))
            stores[-1].start()
    back = jnp.dot(left[...], ratio[...], preferred_element_type=jnp.float32).astype(jnp.bfloat16)
    block_update = lax.dot_general(
        back, right[...], (((1,), (1,)), ((), ())), preferred_element_type=jnp.float32
    ).astype(jnp.bfloat16)
    for here, natural in places:
        leaving[here, :] = block_update[natural, :]
    for c in stores:
        c.wait()


def step(*operands):
    square = jax.ShapeDtypeStruct((SIDE, SIDE), jnp.bfloat16)
    return pl.pallas_call(
        step_kernel,
        out_shape=(square, square, square),
        in_specs=[vmem()] * 6,
        out_specs=(hbm(), hbm(), vmem()),
        scratch_shapes=[pltpu.VMEM((SIDE, SIDE), jnp.bfloat16)] * 4
        + [pltpu.SemaphoreType.DMA((2 * SIDE // STRIP,))],
        compiler_params=pltpu.CompilerParams(vmem_limit_bytes=24 * 1024 * 1024),
        cost_estimate=pl.CostEstimate(
            flops=8 * SIDE**3, bytes_accessed=18 * SIDE**2, transcendentals=2 * SIDE**2
        ),
        name="soap_step",
    )(*operands)


def exchange(pieces):
    return lax.all_to_all(pieces, "fsdp", 0, 0, axis_index_groups=[ORDER], tiled=True)


def exchange_over_x(pair):
    chips = [[2 * chip_of(p) + core for p in range(N_X)] for core in range(2)]
    return lax.all_to_all(pair, "rep", 0, 0, axis_index_groups=chips, tiled=True)


def local(partials, left_basis, right_basis, first_moment, second_moment, owners):
    n_rep = 2 * N_X
    rep = lax.axis_index("rep")
    core = lax.rem(rep, 2)
    owner_row = lax.dynamic_slice_in_dim(owners, rep, 1, 0)[0]
    slots = natural_of(jnp.arange(N_FSDP, dtype=jnp.int32))
    selector = (owner_row[None, :] == slots[:, None]).astype(jnp.bfloat16)
    left = left_basis[0, 0]
    right = right_basis[0, 0]

    own = partials[0]
    other = lax.ppermute(own, "rep", [(i, i ^ 1) for i in range(n_rep)])
    other, left_turned, selector = lax.optimization_barrier((other, left.T, selector))
    pair = add_pair(own, other)
    early = lax.cond(core == 1, exchange_over_x, jnp.zeros_like, pair)
    follow = lax.ppermute(early[0, 0], "rep", [(i + 1, i) for i in range(0, n_rep, 2)])
    pair = add_pair(own, other, follow)
    terms = lax.cond(core == 0, lambda p, e: exchange_over_x(p), lambda p, e: e, pair, early)

    outgoing = jnp.einsum(
        "qt,tsk->qsk",
        jnp.tile(selector, (1, N_X)),
        terms.reshape(N_X * BLOCKS, SUB, SIDE),
        preferred_element_type=jnp.float32,
    ).astype(jnp.bfloat16)
    arrived = exchange(outgoing)
    first_new, second_new, leaving = step(
        arrived.reshape(SIDE, SIDE), left, left_turned, right,
        first_moment[0, 0], second_moment[0, 0],
    )
    returned = exchange(leaving.reshape(N_FSDP, SUB, SIDE))
    update = jnp.einsum(
        "qb,qsk->bsk", selector, returned, preferred_element_type=jnp.float32
    ).astype(jnp.bfloat16)
    return (first_new[None, None], second_new[None, None], update)


def solution(mesh):
    return jax.shard_map(
        local,
        mesh=mesh,
        in_specs=(
            P("rep", None, "fsdp", None),
            P("rep", "fsdp", None, None),
            P("rep", "fsdp", None, None),
            P("rep", "fsdp", None, None),
            P("rep", "fsdp", None, None),
            P(),
        ),
        out_specs=(
            P("rep", "fsdp", None, None),
            P("rep", "fsdp", None, None),
            P(None, "fsdp", "rep"),
        ),
        check_vma=False,
    )
```

```python
import jax
import jax.numpy as jnp
from jax import lax
from jax.experimental import pallas as pl
from jax.experimental.pallas import tpu as pltpu
from jax.sharding import PartitionSpec as P

N_X = 4
N_Y = 4
N_Z = 16
N_FSDP = N_Z * N_Y
SUB = 8
SIDE = 512
BLOCKS = 16
STRIP = 128

def natural_of(p):
    return (p // N_Y + N_Z // 2) % N_Z * N_Y + (p % N_Y + N_Y // 2) % N_Y


def chip_of(p):
    return (p + N_X // 2) % N_X


ORDER = [natural_of(p) for p in range(N_FSDP)]
PAIR = 2 * SUB


def hbm():
    return pl.BlockSpec(memory_space=pl.ANY)


def vmem():
    return pl.BlockSpec(memory_space=pltpu.VMEM)


def pair_kernel(own, other, *refs):
    pair = refs[-1]
    core = lax.rem(lax.axis_index("rep"), 2)
    for p in range(N_X):
        columns = pl.ds(pl.multiple_of((2 * chip_of(p) + core) * SIDE, SIDE), SIDE)
        total = own[:, :, columns].astype(jnp.float32) + other[:, :, columns].astype(jnp.float32)
        pair[p] = total.astype(jnp.bfloat16)


def add_pair(own, other, *after):
    return pl.pallas_call(
        pair_kernel,
        out_shape=jax.ShapeDtypeStruct((N_X, BLOCKS, SUB, SIDE), jnp.bfloat16),
        in_specs=[vmem(), vmem()] + [vmem()] * len(after),
        out_specs=vmem(),
        compiler_params=pltpu.CompilerParams(vmem_limit_bytes=16 * 1024 * 1024),
        name="add_pair",
    )(own, other, *after)


def step_kernel(
    arrived, left, left_turned, right, first, second,
    first_new_hbm, second_new_hbm, leaving,
    grad, first_new, second_new, ratio, sems,
):
    places = [
        (slice(p * SUB, p * SUB + PAIR), slice(ORDER[p] * SUB, ORDER[p] * SUB + PAIR))
        for p in range(0, N_FSDP, 2)
    ]
    for here, natural in places:
        grad[natural, :] = arrived[here, :]
    turned = jnp.dot(left_turned[...], grad[...], preferred_element_type=jnp.float32).astype(
        jnp.bfloat16
    )
    stores = []
    for i in range(SIDE // STRIP):
        rows = slice(i * STRIP, (i + 1) * STRIP)
        rotated = jnp.dot(turned[rows], right[...], preferred_element_type=jnp.float32)
        one = 0.95 * first[rows, :].astype(jnp.float32) + 0.05 * rotated
        two = 0.95 * second[rows, :].astype(jnp.float32) + 0.05 * rotated * rotated
        first_new[rows, :] = one.astype(jnp.bfloat16)
        second_new[rows, :] = two.astype(jnp.bfloat16)
        ratio[rows, :] = (one / (two * lax.rsqrt(two) + 1e-08)).astype(jnp.bfloat16)
        for j, (src, dst) in enumerate(((first_new, first_new_hbm), (second_new, second_new_hbm))):
            part = pl.ds(i * STRIP, STRIP)
            stores.append(pltpu.make_async_copy(src.at[part], dst.at[part], sems.at[2 * i + j]))
            stores[-1].start()
    for low in range(0, SIDE, SIDE // 2):
        high = low + SIDE // 2
        back = jnp.dot(left[low:high, :], ratio[...], preferred_element_type=jnp.float32)
        block_update = lax.dot_general(
            back.astype(jnp.bfloat16),
            right[...],
            (((1,), (1,)), ((), ())),
            preferred_element_type=jnp.float32,
        ).astype(jnp.bfloat16)
        for here, natural in places:
            if low <= natural.start < high:
                leaving[here, :] = block_update[natural.start - low : natural.stop - low]
    for c in stores:
        c.wait()


def step(*operands):
    square = jax.ShapeDtypeStruct((SIDE, SIDE), jnp.bfloat16)
    return pl.pallas_call(
        step_kernel,
        out_shape=(square, square, square),
        in_specs=[vmem()] * 6,
        out_specs=(hbm(), hbm(), vmem()),
        scratch_shapes=[pltpu.VMEM((SIDE, SIDE), jnp.bfloat16)] * 4
        + [pltpu.SemaphoreType.DMA((2 * SIDE // STRIP,))],
        compiler_params=pltpu.CompilerParams(vmem_limit_bytes=24 * 1024 * 1024),
        cost_estimate=pl.CostEstimate(
            flops=8 * SIDE**3, bytes_accessed=18 * SIDE**2, transcendentals=2 * SIDE**2
        ),
        name="soap_step",
    )(*operands)


def exchange(pieces):
    return lax.all_to_all(pieces, "fsdp", 0, 0, axis_index_groups=[ORDER], tiled=True)


def sum_over_x(pair):
    chips = [[2 * chip_of(p) + core for p in range(N_X)] for core in range(2)]
    parts = lax.all_to_all(pair, "rep", 0, 0, axis_index_groups=chips, tiled=True)
    return jnp.sum(parts.astype(jnp.float32), axis=0).astype(jnp.bfloat16)


def local(partials, left_basis, right_basis, first_moment, second_moment, owners):
    n_rep = 2 * N_X
    rep = lax.axis_index("rep")
    core = lax.rem(rep, 2)
    owner_row = lax.dynamic_slice_in_dim(owners, rep, 1, 0)[0]
    slots = natural_of(jnp.arange(N_FSDP, dtype=jnp.int32))
    selector = (owner_row[None, :] == slots[:, None]).astype(jnp.bfloat16)
    left = left_basis[0, 0]
    right = right_basis[0, 0]

    own = partials[0]
    other = lax.ppermute(own, "rep", [(i, i ^ 1) for i in range(n_rep)])
    other, left_turned, selector = lax.optimization_barrier((other, left.T, selector))
    pair = add_pair(own, other)
    early = lax.cond(core == 1, sum_over_x, lambda p: jnp.zeros(p.shape[1:], p.dtype), pair)
    follow = lax.ppermute(early[0], "rep", [(i + 1, i) for i in range(0, n_rep, 2)])
    pair = add_pair(own, other, follow)
    pieces = lax.cond(core == 0, lambda p, e: sum_over_x(p), lambda p, e: e, pair, early)

    outgoing = jnp.einsum(
        "qb,bsk->qsk", selector, pieces, preferred_element_type=jnp.float32
    ).astype(jnp.bfloat16)
    arrived = exchange(outgoing)
    first_new, second_new, leaving = step(
        arrived.reshape(SIDE, SIDE), left, left_turned, right,
        first_moment[0, 0], second_moment[0, 0],
    )
    returned = exchange(leaving.reshape(N_FSDP, SUB, SIDE))
    update = jnp.einsum(
        "qb,qsk->bsk", selector, returned, preferred_element_type=jnp.float32
    ).astype(jnp.bfloat16)
    return (first_new[None, None], second_new[None, None], update)


def solution(mesh):
    return jax.shard_map(
        local,
        mesh=mesh,
        in_specs=(
            P("rep", None, "fsdp", None),
            P("rep", "fsdp", None, None),
            P("rep", "fsdp", None, None),
            P("rep", "fsdp", None, None),
            P("rep", "fsdp", None, None),
            P(),
        ),
        out_specs=(
            P("rep", "fsdp", None, None),
            P("rep", "fsdp", None, None),
            P(None, "fsdp", "rep"),
        ),
        check_vma=False,
    )
```
